256 devices in a mesh: dp: 32 (over y, x, core), vocab: 8 (over z).
Axes of the slice: x: 4, y: 4, z: 8, core: 2. Of those that a mesh axis runs over, the one named last changes fastest.
Arguments:
- embedding: bfloat16 [4096, 4608], P('vocab'), may hold values from -0.36 to 0.36
- hidden: bfloat16 [16384, 4608], P('dp'), may hold values from -2 to 2
- targets: int32 [16384], P('dp'), may hold values from 0 to 4095
- input_ids: int32 [16384], P('dp'), may hold values from 0 to 4095, as said below
- input_grad: bfloat16 [16384, 4608], P('dp', 'vocab'), may hold values from -6 to 6
Outputs:
- token_loss: float32 [16384], P('dp')
- hidden_grad: float32 [16384, 4608], P('dp', 'vocab')
- embed_grad: float32 [4096, 4608], P('vocab', 'dp')
The draws below stay inside these ranges and needn't reach their ends.
Inputs may be any that keep to these rules, and one draw needn't show every extreme that they name: `input_ids`: within each data group's 512 tokens (aligned blocks), at most 256 ids lie in any one vocabulary shard of 512 rows, and some shard holds exactly 256 of them in every group.
All inputs are finite; a program needn't handle non-finite values.
Results may differ from the reference program's by a relative error of at most 0.0018.
Values may be sent and summed in bfloat16 or wider, within the bound.
No kernel may reach another device: no remote copies, remote signals or barrier semaphores. Data moves between devices by JAX's collectives and lax.ppermute only.
A program may use at most 128 MiB of HBM per device.

```python
import jax
import jax.numpy as jnp

D = 4608
VOCAB_DEV = 512
TOK_DEV = 512
VOCAB = 4096
TOKENS = 16384


def draw_input_ids(key, part):
    key = jax.random.fold_in(key, 11)
    key_hot, key_shift, key_perm, key_top, key_off = jax.random.split(key, 5)
    blocks = TOKENS // TOK_DEV
    owners = VOCAB // VOCAB_DEV
    limit = TOK_DEV // 2
    hot_owner = jax.random.randint(key_hot, (blocks, 1), 0, owners)
    shifted = jax.random.randint(key_shift, (blocks, TOK_DEV), 1, owners)
    other_owner = (hot_owner + shifted) % owners
    position = jnp.arange(TOK_DEV, dtype=jnp.int32)[None, :]
    owner_of = jnp.where(position < limit, hot_owner, other_owner)
    perm_keys = jax.random.split(key_perm, blocks)
    owner_of = jax.vmap(lambda k, row: jax.random.permutation(k, row))(perm_keys, owner_of)
    upper = jax.random.randint(key_top, (blocks, TOK_DEV), 1, VOCAB_DEV + 1)
    offset = jax.random.randint(key_off, (blocks, TOK_DEV), 0, upper)
    return (owner_of * VOCAB_DEV + offset).reshape(-1).astype(jnp.int32)


def draw_embedding(key, part):
    key = jax.random.fold_in(key, 21)
    key_noise, key_common = jax.random.split(key)
    noise = 0.06 * jnp.clip(jax.random.normal(key_noise, (VOCAB, D), jnp.float32), -5.0, 5.0)
    common = jax.random.uniform(key_common, (1, D), jnp.float32, -0.04, 0.04)
    return (noise + common).astype(jnp.bfloat16)


def draw_hidden(key, part):
    key = jax.random.fold_in(key, 31)
    key_noise, key_scale = jax.random.split(key)
    noise = jnp.clip(jax.random.normal(key_noise, (TOKENS, D), jnp.float32), -4.0, 4.0)
    row_scale = jnp.exp(jax.random.uniform(key_scale, (TOKENS, 1), jnp.float32, jnp.log(0.1), jnp.log(0.5)))
    return (noise * row_scale).astype(jnp.bfloat16)


def set_ends(result, key, least, top_value):
    longest = result.shape.index(max(result.shape))
    spots = []
    for shift in (0, 1):
        where = [jax.random.randint(jax.random.fold_in(key, axis), (), 0, length) for axis, length in enumerate(result.shape)]
        where[longest] = (where[longest] + shift) % result.shape[longest]
        spots.append(tuple(where))
    return result.at[spots[0]].set(least).at[spots[1]].set(top_value)


def shard_levels(rng, extent, shards, least, high):
    def one(axis_at, blocks):
        heights = jax.random.uniform(jax.random.fold_in(jax.random.fold_in(rng, 6), axis_at), (blocks,), jnp.float32, least / len(shards), high / len(shards))
        return jnp.repeat(jnp.exp(heights), extent[axis_at] // blocks).reshape((-1,) + (1,) * (len(extent) - axis_at - 1))

    gain = one(*shards[0])
    for cut in shards[1:]:
        gain = gain * one(*cut)
    return gain


def bell_draw(own_key, shape, spread, bound, shards=(), kind=jnp.bfloat16):
    drawn = jax.random.normal(own_key, shape, jnp.float32) * spread
    if len(shards) > 0:
        drawn = shard_levels(own_key, shape, shards, -0.22, 0.18) * drawn
    return jnp.clip(drawn, min=-bound, max=bound).astype(kind)


def setup_inputs(seed: int = 0) -> dict:
    keys = jax.random.split(jax.random.key(seed), 6)
    embedding = draw_embedding(jax.random.fold_in(keys[5], 71), 0)
    hidden = draw_hidden(jax.random.fold_in(keys[5], 71), 0)
    targets = set_ends(jax.random.randint(keys[2], (TOKENS,), 0, VOCAB), jax.random.fold_in(keys[2], 1), 0, VOCAB - 1).astype(jnp.int32)
    input_ids = draw_input_ids(jax.random.fold_in(keys[5], 71), 0)
    input_grad = bell_draw(keys[4], (TOKENS, D), 1.0, 6.0, ((0, 32), (1, 8)))
    return dict(embedding=embedding, hidden=hidden, targets=targets, input_ids=input_ids, input_grad=input_grad)


softcap = 30.0


def reference(embedding, hidden, targets, input_ids, input_grad):
    table = embedding.astype(jnp.float32)
    logits = jnp.einsum("td,vd->tv", hidden.astype(jnp.float32), table)
    capped = softcap * jnp.tanh(logits / softcap)
    exponent = jnp.exp(capped)
    denominator = jnp.sum(exponent, axis=1)
    columns = jnp.arange(VOCAB, dtype=jnp.int32)
    target_hit = (columns[None, :] == targets[:, None]).astype(jnp.float32)
    picked = jnp.sum(target_hit * capped, axis=1)
    token_loss = jnp.log(denominator) - picked
    scaled = ((exponent / denominator[:, None] - target_hit) * (1.0 - (capped / softcap) ** 2)).astype(jnp.bfloat16)
    scaled_wide = scaled.astype(jnp.float32)
    hidden_grad = jnp.einsum("tv,vd->td", scaled_wide, table)
    tied_part = jnp.einsum("tv,td->vd", scaled_wide, hidden.astype(jnp.float32))
    input_part = jax.ops.segment_sum(input_grad.astype(jnp.float32), input_ids, num_segments=VOCAB)
    return token_loss, hidden_grad, tied_part + input_part
```

```python
import jax
import jax.numpy as jnp
from jax import lax
from jax.experimental import pallas as pl
from jax.experimental.pallas import tpu as pltpu
from jax.sharding import PartitionSpec as P

softcap = 30.0
bf16, f16, f32 = jnp.bfloat16, jnp.float16, jnp.float32
NZ, NX, NY = 8, 4, 4
DP = NX * NY * 2
emb_scale = 0.5


def z_shift(d):
    return [(i, (i + d) % NZ) for i in range(NZ)]


def z_xor(d):
    return [(i, i ^ d) for i in range(NZ)]


core_swap = [(i, i ^ 1) for i in range(DP)]


def segment_kernel(x_ref, o_ref):
    groups, rows, lanes = x_ref.shape
    cols = rows // 4 - 2
    r_iota = lax.broadcasted_iota(jnp.int32, (256, lanes), 0).astype(f32)
    q_iota = lax.broadcasted_iota(jnp.int32, (16, lanes), 0).astype(f32)

    def body(g, acc):
        x = x_ref[g].astype(f32)
        left, right = [], []
        for k in range(4):
            base = k * (cols + 2)
            hit = x[base + cols : base + cols + 1] == q_iota
            left.append(
                jnp.concatenate(
                    [jnp.where(hit, x[base + c : base + c + 1], 0.0) for c in range(cols)], axis=0
                ).astype(bf16)
            )
            right.append(jnp.where(x[base + cols + 1 : base + cols + 2] == r_iota, 1.0, 0.0).astype(bf16))
        left = jnp.concatenate(left, axis=1)
        right = jnp.concatenate(right, axis=1)
        return acc + lax.dot_general(left, right, (((1,), (1,)), ((), ())), preferred_element_type=f32)

    acc = lax.fori_loop(0, groups, body, jnp.zeros((cols * 16, 256), f32))
    for c in range(cols):
        for q in range(16):
            o_ref[q // 2, c : c + 1, (q % 2) * 256 : (q % 2 + 1) * 256] = acc[c * 16 + q : c * 16 + q + 1]


def segment_sum(x):
    cols = x.shape[1] // 4 - 2
    return pl.pallas_call(
        segment_kernel,
        out_shape=jax.ShapeDtypeStruct((NZ, cols, 512), f32),
        in_specs=[pl.BlockSpec(memory_space=pltpu.VMEM)],
        out_specs=pl.BlockSpec(memory_space=pltpu.VMEM),
        compiler_params=pltpu.CompilerParams(vmem_limit_bytes=24 * 1024 * 1024),
        cost_estimate=pl.CostEstimate(flops=5_000_000_000, bytes_accessed=2_000_000, transcendentals=0),
    )(x)


same_core = [[2 * chip + c for chip in range(DP // 2)] for c in range(2)]
same_core_parity = [[2 * (2 * b + a) + c for b in range(8)] for a in range(2) for c in range(2)]
MB = 1024 * 1024


def after(x, *others):
    return lax.optimization_barrier((x,) + others)[0]


def hid_kernel(blocks, last, *refs):
    at_ref, emb_ref = refs[:2]
    block_refs = refs[2 : 2 + blocks]
    o_ref = refs[-1]
    rows = block_refs[0].shape[1]
    total = refs[2 + blocks][...] if last else None
    for i, block in enumerate(block_refs):
        term = jnp.dot(block[...], emb_ref[:, at_ref[i]].reshape(rows, -1), preferred_element_type=f32)
        total = term if total is None else total + term
    o_ref[...] = total.T if last else total


def hid_terms(emb_cols, shards, blocks, total=None):
    tokens, piece = blocks[0].shape[0], emb_cols.shape[-1]
    last = total is not None
    at = jnp.stack([s % NZ for s in shards])
    vmem = pl.BlockSpec(memory_space=pltpu.VMEM)
    args = [emb_cols, *blocks] + ([total] if last else [])
    return pl.pallas_call(
        lambda *refs: hid_kernel(len(blocks), last, *refs),
        out_shape=jax.ShapeDtypeStruct((piece, tokens) if last else (tokens, piece), f32),
        in_specs=[pl.BlockSpec(memory_space=pltpu.SMEM)] + [vmem] * len(args),
        out_specs=vmem,
        compiler_params=pltpu.CompilerParams(vmem_limit_bytes=28 * MB),
        cost_estimate=pl.CostEstimate(
            flops=2 * len(blocks) * tokens * tokens * piece, bytes_accessed=8 * MB, transcendentals=0
        ),
    )(at, *args)


def split_kernel(core_ref, x_ref, own_ref, other_ref):
    chips, own_cols, tokens = own_ref.shape
    x = x_ref[...].T.reshape(chips, 2, own_cols, tokens)
    first = core_ref[0] == 0
    own_ref[...] = jnp.where(first, x[:, 0], x[:, 1])
    other_ref[...] = jnp.where(first, x[:, 1], x[:, 0])


def split_hidden(hidden, core):
    tokens, width = hidden.shape
    own_cols = width // DP
    out = jax.ShapeDtypeStruct((DP // 2, own_cols, tokens), hidden.dtype)
    spec = pl.BlockSpec((4, own_cols, tokens), lambda i: (i, 0, 0))
    return pl.pallas_call(
        split_kernel,
        grid=(DP // 8,),
        out_shape=(out, out),
        in_specs=[pl.BlockSpec(memory_space=pltpu.SMEM), pl.BlockSpec((tokens, 8 * own_cols), lambda i: (0, i))],
        out_specs=(spec, spec),
        compiler_params=pltpu.CompilerParams(vmem_limit_bytes=24 * MB),
        cost_estimate=pl.CostEstimate(flops=0, bytes_accessed=9 * MB, transcendentals=0),
    )(core[None], hidden)


def per_device(embedding, hidden, targets, input_ids, input_grad):
    vocab_rows, width = embedding.shape
    tokens = hidden.shape[0]
    z = lax.axis_index("vocab")
    dp = lax.axis_index("dp")
    core, chip = dp % 2, dp // 2
    chips = DP // 2
    offset = z * vocab_rows
    piece = width // NZ
    own_cols = width // DP
    cols = piece // DP

    few = vocab_rows // DP
    emb_few = lax.dynamic_slice(embedding, (dp * few, 0), (few, width))
    emb_few = emb_few.reshape(few, NZ, piece).transpose(1, 0, 2)
    emb_few = lax.all_to_all(emb_few, "vocab", 0, 0, tiled=True)

    logits = jnp.einsum("td,vd->tv", hidden, embedding, preferred_element_type=f32)
    capped = softcap * jnp.tanh(logits / softcap)
    exponent = jnp.exp(capped)
    row_index = jnp.arange(vocab_rows, dtype=jnp.int32)
    target_hit = (row_index[None, :] == (targets - offset)[:, None]).astype(f32)
    stats = jnp.stack([jnp.sum(exponent, axis=1), jnp.sum(target_hit * capped, axis=1)])
    stats1 = stats + lax.ppermute(stats, "vocab", z_xor(1))
    emb_cols = lax.all_gather(after(emb_few, stats), "dp", axis=0, tiled=False)
    grad_t = after(input_grad, stats).T.reshape(2, 2, 8, cols, tokens)
    grad_t = grad_t.transpose(2, 0, 1, 3, 4).reshape(DP, cols, tokens)
    digits = jnp.stack([input_ids // 256, input_ids % 256]).astype(bf16)
    packed = jnp.concatenate([grad_t, jnp.broadcast_to(digits[None], (DP, 2, tokens))], axis=1)
    packed = after(packed, stats1).reshape(DP, cols + 2, 4, 128).transpose(0, 2, 1, 3).reshape(DP, 4 * (cols + 2), 128)
    packed = lax.all_to_all(packed, "dp", 0, 0, tiled=True)

    stats2 = stats1 + lax.ppermute(stats1, "vocab", z_xor(2))

    hid_own, hid_other = split_hidden(after(hidden, stats2), core)
    hid_other = lax.ppermute(hid_other, "dp", core_swap)

    hid_pair = jnp.concatenate([hid_own, hid_other], axis=2)

    stats3 = stats2 + lax.ppermute(stats2, "vocab", z_xor(4))
    denominator, picked = stats3[0], stats3[1]
    token_loss = jnp.log(denominator) - picked
    scaled = (
        (exponent / denominator[:, None] - target_hit) * (1.0 - (capped / softcap) ** 2)
    ).astype(bf16)

    up1, down1 = lax.ppermute(scaled, "vocab", z_shift(1)), lax.ppermute(scaled, "vocab", z_shift(-1))
    scaled_other = lax.ppermute(scaled, "dp", core_swap)

    up2, down2 = lax.ppermute(up1, "vocab", z_shift(1)), lax.ppermute(down1, "vocab", z_shift(-1))

    tied = jnp.einsum("kdt,tv->kdv", hid_pair, jnp.concatenate([scaled, scaled_other]), preferred_element_type=f32)
    tied = after((tied * emb_scale).astype(f16), up1, down1)
    tied = lax.all_to_all(tied, "dp", 0, 0, axis_index_groups=same_core, tiled=True)

    up3, down3 = lax.ppermute(up2, "vocab", z_shift(1)), lax.ppermute(down2, "vocab", z_shift(-1))

    sums = segment_sum(after(packed, up1, down1))
    sums = (sums * emb_scale).astype(f16).reshape(NZ, cols * vocab_rows // 128, 128)
    sums = lax.all_to_all(after(sums, tied), "vocab", 0, 0, tiled=True)

    half = tokens // 2
    up4, down4 = lax.ppermute(up3[:half], "vocab", z_shift(1)), lax.ppermute(down3[half:], "vocab", z_shift(-1))
    sums = lax.all_to_all(sums, "dp", 0, 0, axis_index_groups=same_core_parity, tiled=True)
    sums = sums.reshape(own_cols, vocab_rows)

    hid_sum = hid_terms(
        emb_cols, [z, z + 7, z + 1, z + 6, z + 2], [scaled, up1, down1, up2, down2]
    )
    hidden_grad = hid_terms(
        emb_cols, [z + 5, z + 3, z + 4], [up3, down3, jnp.concatenate([up4, down4], axis=0)], hid_sum
    ).T

    embed_grad = ((jnp.sum(tied.astype(f32), axis=0) + sums.astype(f32)) * (1.0 / emb_scale)).T
    return (token_loss, hidden_grad, embed_grad)


def solution(mesh):
    return jax.shard_map(
        per_device,
        mesh=mesh,
        in_specs=(P("vocab", None), P("dp", None), P("dp"), P("dp"), P("dp", "vocab")),
        out_specs=(P("dp"), P("dp", "vocab"), P("vocab", "dp")),
        check_vma=False,
    )
```

```python
import jax
import jax.numpy as jnp
from jax import lax
from jax.experimental import pallas as pl
from jax.experimental.pallas import tpu as pltpu
from jax.sharding import PartitionSpec as P

softcap = 30.0
bf16, f16, f32 = jnp.bfloat16, jnp.float16, jnp.float32
NZ, NX, NY = 8, 4, 4
DP = NX * NY * 2
emb_scale = 0.5


def z_shift(d):
    return [(i, (i + d) % NZ) for i in range(NZ)]


def z_xor(d):
    return [(i, i ^ d) for i in range(NZ)]


core_swap = [(i, i ^ 1) for i in range(DP)]


def segment_kernel(x_ref, o_ref):
    groups, rows, lanes = x_ref.shape
    cols = rows // 4 - 2
    r_iota = lax.broadcasted_iota(jnp.int32, (256, lanes), 0).astype(f32)
    q_iota = lax.broadcasted_iota(jnp.int32, (16, lanes), 0).astype(f32)

    def body(step, acc):
        left, right = [], []
        for n in range(4):
            x = x_ref[4 * step + n].astype(f32)
            for k in range(4):
                base = k * (cols + 2)
                hit = x[base + cols : base + cols + 1] == q_iota
                left.append(
                    jnp.concatenate(
                        [jnp.where(hit, x[base + c : base + c + 1], 0.0) for c in range(cols)], axis=0
                    ).astype(bf16)
                )
                right.append(jnp.where(x[base + cols + 1 : base + cols + 2] == r_iota, 1.0, 0.0).astype(bf16))
        left = jnp.concatenate(left, axis=1)
        right = jnp.concatenate(right, axis=1)
        return acc + lax.dot_general(left, right, (((1,), (1,)), ((), ())), preferred_element_type=f32)

    acc = lax.fori_loop(0, groups // 4, body, jnp.zeros((cols * 16, 256), f32))
    for c in range(cols):
        for q in range(16):
            o_ref[q // 2, c : c + 1, (q % 2) * 256 : (q % 2 + 1) * 256] = acc[c * 16 + q : c * 16 + q + 1]


def segment_sum(x):
    cols = x.shape[1] // 4 - 2
    return pl.pallas_call(
        segment_kernel,
        out_shape=jax.ShapeDtypeStruct((NZ, cols, 512), f32),
        in_specs=[pl.BlockSpec(memory_space=pltpu.VMEM)],
        out_specs=pl.BlockSpec(memory_space=pltpu.VMEM),
        compiler_params=pltpu.CompilerParams(vmem_limit_bytes=24 * 1024 * 1024),
        cost_estimate=pl.CostEstimate(flops=5_000_000_000, bytes_accessed=2_000_000, transcendentals=0),
    )(x)


same_core = [[2 * chip + c for chip in range(DP // 2)] for c in range(2)]
MB = 1024 * 1024


def after(x, *others):
    return lax.optimization_barrier((x,) + others)[0]


def hid_kernel(blocks, last, *refs):
    at_ref, emb_ref = refs[:2]
    block_refs = refs[2 : 2 + blocks]
    o_ref = refs[-1]
    rows = block_refs[0].shape[1]
    total = refs[2 + blocks][...] if last else None
    for i, block in enumerate(block_refs):
        term = jnp.dot(block[...], emb_ref[:, at_ref[i]].reshape(rows, -1), preferred_element_type=f32)
        total = term if total is None else total + term
    o_ref[...] = total.T if last else total


def hid_terms(emb_cols, shards, blocks, total=None):
    tokens, piece = blocks[0].shape[0], emb_cols.shape[-1]
    last = total is not None
    at = jnp.stack([s % NZ for s in shards])
    vmem = pl.BlockSpec(memory_space=pltpu.VMEM)
    args = [emb_cols, *blocks] + ([total] if last else [])
    return pl.pallas_call(
        lambda *refs: hid_kernel(len(blocks), last, *refs),
        out_shape=jax.ShapeDtypeStruct((piece, tokens) if last else (tokens, piece), f32),
        in_specs=[pl.BlockSpec(memory_space=pltpu.SMEM)] + [vmem] * len(args),
        out_specs=vmem,
        compiler_params=pltpu.CompilerParams(vmem_limit_bytes=28 * MB),
        cost_estimate=pl.CostEstimate(
            flops=2 * len(blocks) * tokens * tokens * piece, bytes_accessed=8 * MB, transcendentals=0
        ),
    )(at, *args)


def pack_kernel(grad_ref, ids_ref, o_ref):
    cols = o_ref.shape[1] // 4 - 2
    grad = grad_ref[...].astype(f32)
    ids = ids_ref[...]
    digits = [(ids // 256).astype(f32), (ids % 256).astype(f32)]
    for device in range(DP):
        b, a, c = device // 4, device // 2 % 2, device % 2
        base = ((a * 2 + c) * 8 + b) * cols
        rows = []
        for k in range(4):
            lanes = slice(k * 128, (k + 1) * 128)
            rows += [grad[base : base + cols, lanes]] + [d[:, lanes] for d in digits]
        o_ref[device] = jnp.concatenate(rows, axis=0).astype(bf16)


def pack_input(grad_t, ids):
    piece, tokens = grad_t.shape
    vmem = pl.BlockSpec(memory_space=pltpu.VMEM)
    return pl.pallas_call(
        pack_kernel,
        out_shape=jax.ShapeDtypeStruct((DP, 4 * (piece // DP + 2), tokens // 4), bf16),
        in_specs=[vmem, vmem],
        out_specs=vmem,
        compiler_params=pltpu.CompilerParams(vmem_limit_bytes=16 * MB),
        cost_estimate=pl.CostEstimate(flops=0, bytes_accessed=2 * MB, transcendentals=0),
    )(grad_t, ids.reshape(1, tokens))


def split_kernel(core_ref, x_ref, own_ref, other_ref):
    chips, own_cols, tokens = own_ref.shape
    x = x_ref[...].T.reshape(chips, 2, own_cols, tokens)
    first = core_ref[0] == 0
    own_ref[...] = jnp.where(first, x[:, 0], x[:, 1])
    other_ref[...] = jnp.where(first, x[:, 1], x[:, 0])


def split_hidden(hidden, core):
    tokens, width = hidden.shape
    own_cols = width // DP
    out = jax.ShapeDtypeStruct((DP // 2, own_cols, tokens), hidden.dtype)
    spec = pl.BlockSpec((4, own_cols, tokens), lambda i: (i, 0, 0))
    return pl.pallas_call(
        split_kernel,
        grid=(DP // 8,),
        out_shape=(out, out),
        in_specs=[pl.BlockSpec(memory_space=pltpu.SMEM), pl.BlockSpec((tokens, 8 * own_cols), lambda i: (0, i))],
        out_specs=(spec, spec),
        compiler_params=pltpu.CompilerParams(vmem_limit_bytes=24 * MB),
        cost_estimate=pl.CostEstimate(flops=0, bytes_accessed=9 * MB, transcendentals=0),
    )(core[None], hidden)


def per_device(embedding, hidden, targets, input_ids, input_grad):
    vocab_rows, width = embedding.shape
    tokens = hidden.shape[0]
    z = lax.axis_index("vocab")
    dp = lax.axis_index("dp")
    core, chip = dp % 2, dp // 2
    chips = DP // 2
    offset = z * vocab_rows
    piece = width // NZ
    own_cols = width // DP
    cols = piece // DP

    few = vocab_rows // DP
    emb_few = lax.dynamic_slice(embedding, (dp * few, 0), (few, width))
    emb_few = emb_few.reshape(few, NZ, piece).transpose(1, 0, 2)
    emb_few = lax.all_to_all(emb_few, "vocab", 0, 0, tiled=True)

    logits = jnp.einsum("td,vd->tv", hidden, embedding, preferred_element_type=f32)
    capped = softcap * jnp.tanh(logits / softcap)
    exponent = jnp.exp(capped)
    row_index = jnp.arange(vocab_rows, dtype=jnp.int32)
    target_hit = (row_index[None, :] == (targets - offset)[:, None]).astype(f32)
    stats = jnp.stack([jnp.sum(exponent, axis=1), jnp.sum(target_hit * capped, axis=1)])
    stats1 = stats + lax.ppermute(stats, "vocab", z_xor(1))
    emb_cols = lax.all_gather(after(emb_few, stats), "dp", axis=0, tiled=False)
    packed = pack_input(after(input_grad, stats).T, input_ids)
    stats1 = after(stats1, packed)
    stats2 = stats1 + lax.ppermute(stats1, "vocab", z_xor(2))
    packed = lax.all_to_all(packed, "dp", 0, 0, tiled=True)

    stats3 = stats2 + lax.ppermute(stats2, "vocab", z_xor(4))
    stats3 = after(stats3, packed)
    denominator, picked = stats3[0], stats3[1]
    token_loss = jnp.log(denominator) - picked
    scaled = (
        (exponent / denominator[:, None] - target_hit) * (1.0 - (capped / softcap) ** 2)
    ).astype(bf16)

    up1, down1 = lax.ppermute(scaled, "vocab", z_shift(1)), lax.ppermute(scaled, "vocab", z_shift(-1))
    scaled_other = lax.ppermute(scaled, "dp", core_swap)

    hid_own, hid_other = split_hidden(after(hidden, stats2), core)
    hid_other = lax.ppermute(hid_other, "dp", core_swap)
    row = lax.broadcasted_iota(jnp.int32, (chips * own_cols, 2 * NZ * cols), 0)
    term = lax.broadcasted_iota(jnp.int32, (chips * own_cols, 2 * NZ * cols), 1) % (NZ * cols)
    place = (2 * (term // cols) + chip % 2) * own_cols + chip // 2 * cols + term % cols
    place = jnp.where(row == place, 1.0 / emb_scale, 0.0).astype(bf16).reshape(chips, own_cols, 2 * NZ * cols)
    hid_pair = jnp.concatenate([hid_own, hid_other, place], axis=2)

    up2, down2 = lax.ppermute(up1, "vocab", z_shift(1)), lax.ppermute(down1, "vocab", z_shift(-1))

    sums = segment_sum(after(packed, up1, down1))
    sums = (sums * emb_scale).astype(f16).reshape(NZ, cols * vocab_rows // 128, 128)
    sums = lax.all_to_all(after(sums, up1, down1), "vocab", 0, 0, tiled=True).reshape(NZ * cols, vocab_rows)
    sums_high = sums.astype(bf16)
    sums_low = (sums.astype(f32) - sums_high.astype(f32)).astype(bf16)

    up3, down3 = lax.ppermute(up2, "vocab", z_shift(1)), lax.ppermute(down2, "vocab", z_shift(-1))

    sums_high = after(sums_high, up2, down2)
    terms = jnp.concatenate([scaled, scaled_other, sums_high, sums_low])
    tied = jnp.einsum("kdt,tv->kdv", hid_pair, terms, preferred_element_type=f32)
    tied = (tied * emb_scale).astype(f16)
    tied = lax.all_to_all(tied, "dp", 0, 0, axis_index_groups=same_core, tiled=True)

    half = tokens // 2
    up4, down4 = lax.ppermute(up3[:half], "vocab", z_shift(1)), lax.ppermute(down3[half:], "vocab", z_shift(-1))
    hid_sum = hid_terms(
        emb_cols, [z, z + 7, z + 1, z + 6, z + 2], [scaled, up1, down1, up2, down2]
    )
    hidden_grad = hid_terms(
        emb_cols, [z + 5, z + 3, z + 4], [up3, down3, jnp.concatenate([up4, down4], axis=0)], hid_sum
    ).T

    embed_grad = (jnp.sum(after(tied, hidden_grad).astype(f32), axis=0) * (1.0 / emb_scale)).T
    return (token_loss, hidden_grad, embed_grad)


def solution(mesh):
    return jax.shard_map(
        per_device,
        mesh=mesh,
        in_specs=(P("vocab", None), P("dp", None), P("dp"), P("dp"), P("dp", "vocab")),
        out_specs=(P("dp"), P("dp", "vocab"), P("vocab", "dp")),
        check_vma=False,
    )
```

```python
import jax
import jax.numpy as jnp
from jax import lax
from jax.experimental import pallas as pl
from jax.experimental.pallas import tpu as pltpu
from jax.sharding import PartitionSpec as P

softcap = 30.0
bf16, f16, f32 = jnp.bfloat16, jnp.float16, jnp.float32
NZ, NX, NY = 8, 4, 4
DP = NX * NY * 2
emb_scale = 0.5


def z_shift(d):
    return [(i, (i + d) % NZ) for i in range(NZ)]


def z_xor(d):
    return [(i, i ^ d) for i in range(NZ)]


core_swap = [(i, i ^ 1) for i in range(DP)]


def segment_kernel(x_ref, o_ref):
    groups, rows, lanes = x_ref.shape
    cols = rows // 4 - 2
    r_iota = lax.broadcasted_iota(jnp.int32, (256, lanes), 0).astype(f32)
    q_iota = lax.broadcasted_iota(jnp.int32, (16, lanes), 0).astype(f32)

    def body(step, acc):
        left, right = [], []
        for n in range(4):
            x = x_ref[4 * step + n].astype(f32)
            for k in range(4):
                base = k * (cols + 2)
                hit = x[base + cols : base + cols + 1] == q_iota
                left.append(
                    jnp.concatenate(
                        [jnp.where(hit, x[base + c : base + c + 1], 0.0) for c in range(cols)], axis=0
                    ).astype(bf16)
                )
                right.append(jnp.where(x[base + cols + 1 : base + cols + 2] == r_iota, 1.0, 0.0).astype(bf16))
        left = jnp.concatenate(left, axis=1)
        right = jnp.concatenate(right, axis=1)
        return acc + lax.dot_general(left, right, (((1,), (1,)), ((), ())), preferred_element_type=f32)

    acc = lax.fori_loop(0, groups // 4, body, jnp.zeros((cols * 16, 256), f32))
    for c in range(cols):
        for q in range(16):
            o_ref[q // 2, c : c + 1, (q % 2) * 256 : (q % 2 + 1) * 256] = acc[c * 16 + q : c * 16 + q + 1]


def segment_sum(x):
    cols = x.shape[1] // 4 - 2
    return pl.pallas_call(
        segment_kernel,
        out_shape=jax.ShapeDtypeStruct((NZ, cols, 512), f32),
        in_specs=[pl.BlockSpec(memory_space=pltpu.VMEM)],
        out_specs=pl.BlockSpec(memory_space=pltpu.VMEM),
        compiler_params=pltpu.CompilerParams(vmem_limit_bytes=24 * 1024 * 1024),
        cost_estimate=pl.CostEstimate(flops=5_000_000_000, bytes_accessed=2_000_000, transcendentals=0),
    )(x)


same_core = [[2 * chip + c for chip in range(DP // 2)] for c in range(2)]
MB = 1024 * 1024


def after(x, *others):
    return lax.optimization_barrier((x,) + others)[0]


def hid_kernel(blocks, last, *refs):
    at_ref, emb_ref = refs[:2]
    block_refs = refs[2 : 2 + blocks]
    o_ref = refs[-1]
    rows = block_refs[0].shape[1]
    total = refs[2 + blocks][...] if last else None
    for i, block in enumerate(block_refs):
        term = jnp.dot(block[...], emb_ref[:, at_ref[i]].reshape(rows, -1), preferred_element_type=f32)
        total = term if total is None else total + term
    o_ref[...] = total.T if last else total


def hid_terms(emb_cols, shards, blocks, total=None):
    tokens, piece = blocks[0].shape[0], emb_cols.shape[-1]
    last = total is not None
    at = jnp.stack([s % NZ for s in shards])
    vmem = pl.BlockSpec(memory_space=pltpu.VMEM)
    args = [emb_cols, *blocks] + ([total] if last else [])
    return pl.pallas_call(
        lambda *refs: hid_kernel(len(blocks), last, *refs),
        out_shape=jax.ShapeDtypeStruct((piece, tokens) if last else (tokens, piece), f32),
        in_specs=[pl.BlockSpec(memory_space=pltpu.SMEM)] + [vmem] * len(args),
        out_specs=vmem,
        compiler_params=pltpu.CompilerParams(vmem_limit_bytes=28 * MB),
        cost_estimate=pl.CostEstimate(
            flops=2 * len(blocks) * tokens * tokens * piece, bytes_accessed=8 * MB, transcendentals=0
        ),
    )(at, *args)


def pack_kernel(grad_ref, ids_ref, o_ref):
    cols = o_ref.shape[1] // 4 - 2
    grad = grad_ref[...].astype(f32)
    ids = ids_ref[...]
    digits = [(ids // 256).astype(f32), (ids % 256).astype(f32)]
    for device in range(DP):
        b, a, c = device // 4, device // 2 % 2, device % 2
        base = ((a * 2 + c) * 8 + b) * cols
        rows = []
        for k in range(4):
            lanes = slice(k * 128, (k + 1) * 128)
            rows += [grad[base : base + cols, lanes]] + [d[:, lanes] for d in digits]
        o_ref[device] = jnp.concatenate(rows, axis=0).astype(bf16)


def pack_input(grad_t, ids):
    piece, tokens = grad_t.shape
    vmem = pl.BlockSpec(memory_space=pltpu.VMEM)
    return pl.pallas_call(
        pack_kernel,
        out_shape=jax.ShapeDtypeStruct((DP, 4 * (piece // DP + 2), tokens // 4), bf16),
        in_specs=[vmem, vmem],
        out_specs=vmem,
        compiler_params=pltpu.CompilerParams(vmem_limit_bytes=16 * MB),
        cost_estimate=pl.CostEstimate(flops=0, bytes_accessed=2 * MB, transcendentals=0),
    )(grad_t, ids.reshape(1, tokens))


def split_kernel(core_ref, x_ref, own_ref, other_ref):
    chips, own_cols, tokens = own_ref.shape
    x = x_ref[...].T.reshape(chips, 2, own_cols, tokens)
    first = core_ref[0] == 0
    own_ref[...] = jnp.where(first, x[:, 0], x[:, 1])
    other_ref[...] = jnp.where(first, x[:, 1], x[:, 0])


def split_hidden(hidden, core):
    tokens, width = hidden.shape
    own_cols = width // DP
    out = jax.ShapeDtypeStruct((DP // 2, own_cols, tokens), hidden.dtype)
    spec = pl.BlockSpec((4, own_cols, tokens), lambda i: (i, 0, 0))
    return pl.pallas_call(
        split_kernel,
        grid=(DP // 8,),
        out_shape=(out, out),
        in_specs=[pl.BlockSpec(memory_space=pltpu.SMEM), pl.BlockSpec((tokens, 8 * own_cols), lambda i: (0, i))],
        out_specs=(spec, spec),
        compiler_params=pltpu.CompilerParams(vmem_limit_bytes=24 * MB),
        cost_estimate=pl.CostEstimate(flops=0, bytes_accessed=9 * MB, transcendentals=0),
    )(core[None], hidden)


def per_device(embedding, hidden, targets, input_ids, input_grad):
    vocab_rows, width = embedding.shape
    tokens = hidden.shape[0]
    z = lax.axis_index("vocab")
    dp = lax.axis_index("dp")
    core, chip = dp % 2, dp // 2
    chips = DP // 2
    offset = z * vocab_rows
    piece = width // NZ
    own_cols = width // DP
    cols = piece // DP

    few = vocab_rows // DP
    emb_few = lax.dynamic_slice(embedding, (dp * few, 0), (few, width))
    emb_few = emb_few.reshape(few, NZ, piece).transpose(1, 0, 2)
    emb_few = lax.all_to_all(emb_few, "vocab", 0, 0, tiled=True)

    logits = jnp.einsum("td,vd->tv", hidden, embedding, preferred_element_type=f32)
    capped = softcap * jnp.tanh(logits / softcap)
    exponent = jnp.exp(capped)
    row_index = jnp.arange(vocab_rows, dtype=jnp.int32)
    target_hit = (row_index[None, :] == (targets - offset)[:, None]).astype(f32)
    stats = jnp.stack([jnp.sum(exponent, axis=1), jnp.sum(target_hit * capped, axis=1)])
    stats1 = stats + lax.ppermute(stats, "vocab", z_xor(1))
    emb_cols = lax.all_gather(after(emb_few, stats), "dp", axis=0, tiled=False)
    packed = pack_input(after(input_grad, stats).T, input_ids)
    stats1 = after(stats1, packed)
    stats2 = stats1 + lax.ppermute(stats1, "vocab", z_xor(2))
    packed = lax.all_to_all(packed, "dp", 0, 0, tiled=True)

    stats3 = stats2 + lax.ppermute(stats2, "vocab", z_xor(4))
    stats3 = after(stats3, packed)
    denominator, picked = stats3[0], stats3[1]
    token_loss = jnp.log(denominator) - picked
    scaled = (
        (exponent / denominator[:, None] - target_hit) * (1.0 - (capped / softcap) ** 2)
    ).astype(bf16)

    up1, down1 = lax.ppermute(scaled, "vocab", z_shift(1)), lax.ppermute(scaled, "vocab", z_shift(-1))
    scaled_other = lax.ppermute(scaled, "dp", core_swap)

    hid_own, hid_other = split_hidden(after(hidden, stats2), core)
    hid_other = lax.ppermute(hid_other, "dp", core_swap)
    row = lax.broadcasted_iota(jnp.int32, (chips * own_cols, 2 * NZ * cols), 0)
    term = lax.broadcasted_iota(jnp.int32, (chips * own_cols, 2 * NZ * cols), 1) % (NZ * cols)
    place = (2 * (term // cols) + chip % 2) * own_cols + chip // 2 * cols + term % cols
    place = jnp.where(row == place, 1.0 / emb_scale, 0.0).astype(bf16).reshape(chips, own_cols, 2 * NZ * cols)
    hid_pair = jnp.concatenate([hid_own, hid_other, place], axis=2)

    up2, down2 = lax.ppermute(up1, "vocab", z_shift(1)), lax.ppermute(down1, "vocab", z_shift(-1))

    sums = segment_sum(after(packed, hid_own, scaled))
    sums = (sums * emb_scale).astype(f16).reshape(NZ, cols * vocab_rows // 128, 128)
    sums = lax.all_to_all(after(sums, up1, down1), "vocab", 0, 0, tiled=True).reshape(NZ * cols, vocab_rows)
    sums_high = sums.astype(bf16)
    sums_low = (sums.astype(f32) - sums_high.astype(f32)).astype(bf16)

    hid_sum = hid_terms(
        emb_cols, [z, z + 7, z + 1, z + 6, z + 2], [scaled, up1, down1, up2, down2]
    )
    up3 = lax.ppermute(up2, "vocab", z_shift(1))
    down3 = lax.ppermute(after(down2, hid_sum), "vocab", z_shift(-1))

    terms = jnp.concatenate([scaled, scaled_other, sums_high, sums_low])
    tied = jnp.einsum("kdt,tv->kdv", hid_pair, terms, preferred_element_type=f32)
    tied = after((tied * emb_scale).astype(f16), up2, down2)
    tied = lax.all_to_all(tied, "dp", 0, 0, axis_index_groups=same_core, tiled=True)

    half = tokens // 2
    up4, down4 = lax.ppermute(up3[:half], "vocab", z_shift(1)), lax.ppermute(down3[half:], "vocab", z_shift(-1))
    hidden_grad = hid_terms(
        emb_cols, [z + 5, z + 3, z + 4], [up3, down3, jnp.concatenate([up4, down4], axis=0)], hid_sum
    ).T

    embed_grad = (jnp.sum(after(tied, hidden_grad).astype(f32), axis=0) * (1.0 / emb_scale)).T
    return (token_loss, hidden_grad, embed_grad)


def solution(mesh):
    return jax.shard_map(
        per_device,
        mesh=mesh,
        in_specs=(P("vocab", None), P("dp", None), P("dp"), P("dp"), P("dp", "vocab")),
        out_specs=(P("dp"), P("dp", "vocab"), P("vocab", "dp")),
        check_vma=False,
    )
```

```python
import jax
import jax.numpy as jnp
from jax import lax
from jax.experimental import pallas as pl
from jax.experimental.pallas import tpu as pltpu
from jax.sharding import PartitionSpec as P

softcap = 30.0
bf16, f16, f32 = jnp.bfloat16, jnp.float16, jnp.float32
NZ, NX, NY = 8, 4, 4
DP = NX * NY * 2
emb_scale = 0.5


def z_shift(d):
    return [(i, (i + d) % NZ) for i in range(NZ)]


def z_xor(d):
    return [(i, i ^ d) for i in range(NZ)]


core_swap = [(i, i ^ 1) for i in range(DP)]


def segment_kernel(x_ref, o_ref):
    groups, rows, lanes = x_ref.shape
    cols = rows // 4 - 2
    r_iota = lax.broadcasted_iota(jnp.int32, (256, lanes), 0).astype(f32)
    q_iota = lax.broadcasted_iota(jnp.int32, (16, lanes), 0).astype(f32)

    def body(step, acc):
        left, right = [], []
        for n in range(4):
            x = x_ref[4 * step + n].astype(f32)
            for k in range(4):
                base = k * (cols + 2)
                hit = x[base + cols : base + cols + 1] == q_iota
                left.append(
                    jnp.concatenate(
                        [jnp.where(hit, x[base + c : base + c + 1], 0.0) for c in range(cols)], axis=0
                    ).astype(bf16)
                )
                right.append(jnp.where(x[base + cols + 1 : base + cols + 2] == r_iota, 1.0, 0.0).astype(bf16))
        left = jnp.concatenate(left, axis=1)
        right = jnp.concatenate(right, axis=1)
        return acc + lax.dot_general(left, right, (((1,), (1,)), ((), ())), preferred_element_type=f32)

    acc = lax.fori_loop(0, groups // 4, body, jnp.zeros((cols * 16, 256), f32))
    for c in range(cols):
        for q in range(16):
            o_ref[q // 2, c : c + 1, (q % 2) * 256 : (q % 2 + 1) * 256] = acc[c * 16 + q : c * 16 + q + 1]


def segment_sum(x):
    cols = x.shape[1] // 4 - 2
    return pl.pallas_call(
        segment_kernel,
        out_shape=jax.ShapeDtypeStruct((NZ, cols, 512), f32),
        in_specs=[pl.BlockSpec(memory_space=pltpu.VMEM)],
        out_specs=pl.BlockSpec(memory_space=pltpu.VMEM),
        compiler_params=pltpu.CompilerParams(vmem_limit_bytes=24 * 1024 * 1024),
        cost_estimate=pl.CostEstimate(flops=5_000_000_000, bytes_accessed=2_000_000, transcendentals=0),
    )(x)


same_core = [[2 * chip + c for chip in range(DP // 2)] for c in range(2)]
MB = 1024 * 1024


def after(x, *others):
    return lax.optimization_barrier((x,) + others)[0]


def hid_kernel(blocks, last, *refs):
    at_ref, emb_ref = refs[:2]
    block_refs = refs[2 : 2 + blocks]
    o_ref = refs[-1]
    rows = block_refs[0].shape[1]
    total = refs[2 + blocks][...] if last else None
    for i, block in enumerate(block_refs):
        term = jnp.dot(block[...], emb_ref[:, at_ref[i]].reshape(rows, -1), preferred_element_type=f32)
        total = term if total is None else total + term
    o_ref[...] = total.T if last else total


def hid_terms(emb_cols, shards, blocks, total=None):
    tokens, piece = blocks[0].shape[0], emb_cols.shape[-1]
    last = total is not None
    at = jnp.stack([s % NZ for s in shards])
    vmem = pl.BlockSpec(memory_space=pltpu.VMEM)
    args = [emb_cols, *blocks] + ([total] if last else [])
    return pl.pallas_call(
        lambda *refs: hid_kernel(len(blocks), last, *refs),
        out_shape=jax.ShapeDtypeStruct((piece, tokens) if last else (tokens, piece), f32),
        in_specs=[pl.BlockSpec(memory_space=pltpu.SMEM)] + [vmem] * len(args),
        out_specs=vmem,
        compiler_params=pltpu.CompilerParams(vmem_limit_bytes=28 * MB),
        cost_estimate=pl.CostEstimate(
            flops=2 * len(blocks) * tokens * tokens * piece, bytes_accessed=8 * MB, transcendentals=0
        ),
    )(at, *args)


def pack_kernel(grad_ref, ids_ref, o_ref):
    cols = o_ref.shape[1] // 4 - 2
    grad = grad_ref[...].astype(f32)
    ids = ids_ref[...]
    digits = [(ids // 256).astype(f32), (ids % 256).astype(f32)]
    for device in range(DP):
        b, a, c = device // 4, device // 2 % 2, device % 2
        base = ((a * 2 + c) * 8 + b) * cols
        rows = []
        for k in range(4):
            lanes = slice(k * 128, (k + 1) * 128)
            rows += [grad[base : base + cols, lanes]] + [d[:, lanes] for d in digits]
        o_ref[device] = jnp.concatenate(rows, axis=0).astype(bf16)


def pack_input(grad_t, ids):
    piece, tokens = grad_t.shape
    vmem = pl.BlockSpec(memory_space=pltpu.VMEM)
    return pl.pallas_call(
        pack_kernel,
        out_shape=jax.ShapeDtypeStruct((DP, 4 * (piece // DP + 2), tokens // 4), bf16),
        in_specs=[vmem, vmem],
        out_specs=vmem,
        compiler_params=pltpu.CompilerParams(vmem_limit_bytes=16 * MB),
        cost_estimate=pl.CostEstimate(flops=0, bytes_accessed=2 * MB, transcendentals=0),
    )(grad_t, ids.reshape(1, tokens))


def split_kernel(core_ref, x_ref, own_ref, other_ref):
    chips, own_cols, tokens = own_ref.shape
    x = x_ref[...].T.reshape(chips, 2, own_cols, tokens)
    first = core_ref[0] == 0
    own_ref[...] = jnp.where(first, x[:, 0], x[:, 1])
    other_ref[...] = jnp.where(first, x[:, 1], x[:, 0])


def split_hidden(hidden, core):
    tokens, width = hidden.shape
    own_cols = width // DP
    out = jax.ShapeDtypeStruct((DP // 2, own_cols, tokens), hidden.dtype)
    spec = pl.BlockSpec((4, own_cols, tokens), lambda i: (i, 0, 0))
    return pl.pallas_call(
        split_kernel,
        grid=(DP // 8,),
        out_shape=(out, out),
        in_specs=[pl.BlockSpec(memory_space=pltpu.SMEM), pl.BlockSpec((tokens, 8 * own_cols), lambda i: (0, i))],
        out_specs=(spec, spec),
        compiler_params=pltpu.CompilerParams(vmem_limit_bytes=24 * MB),
        cost_estimate=pl.CostEstimate(flops=0, bytes_accessed=9 * MB, transcendentals=0),
    )(core[None], hidden)


def per_device(embedding, hidden, targets, input_ids, input_grad):
    vocab_rows, width = embedding.shape
    tokens = hidden.shape[0]
    z = lax.axis_index("vocab")
    dp = lax.axis_index("dp")
    core, chip = dp % 2, dp // 2
    chips = DP // 2
    offset = z * vocab_rows
    piece = width // NZ
    own_cols = width // DP
    cols = piece // DP

    few = vocab_rows // DP
    emb_few = lax.dynamic_slice(embedding, (dp * few, 0), (few, width))
    emb_few = emb_few.reshape(few, NZ, piece).transpose(1, 0, 2)
    emb_few = lax.all_to_all(emb_few, "vocab", 0, 0, tiled=True)

    logits = jnp.einsum("td,vd->tv", hidden, embedding, preferred_element_type=f32)
    capped = softcap * jnp.tanh(logits / softcap)
    exponent = jnp.exp(capped)
    row_index = jnp.arange(vocab_rows, dtype=jnp.int32)
    target_hit = (row_index[None, :] == (targets - offset)[:, None]).astype(f32)
    stats = jnp.stack([jnp.sum(exponent, axis=1), jnp.sum(target_hit * capped, axis=1)])
    stats1 = stats + lax.ppermute(stats, "vocab", z_xor(1))
    emb_cols = lax.all_gather(after(emb_few, stats), "dp", axis=0, tiled=False)
    packed = pack_input(after(input_grad, stats).T, input_ids)
    stats1 = after(stats1, packed)
    stats2 = stats1 + lax.ppermute(stats1, "vocab", z_xor(2))
    packed = lax.all_to_all(packed, "dp", 0, 0, tiled=True)

    stats3 = stats2 + lax.ppermute(stats2, "vocab", z_xor(4))
    stats3 = after(stats3, packed)
    denominator, picked = stats3[0], stats3[1]
    token_loss = jnp.log(denominator) - picked
    scaled = (
        (exponent / denominator[:, None] - target_hit) * (1.0 - (capped / softcap) ** 2)
    ).astype(bf16)

    up1, down1 = lax.ppermute(scaled, "vocab", z_shift(1)), lax.ppermute(scaled, "vocab", z_shift(-1))
    scaled_other = lax.ppermute(scaled, "dp", core_swap)

    hid_own, hid_other = split_hidden(after(hidden, stats2), core)
    hid_other = lax.ppermute(hid_other, "dp", core_swap)
    row = lax.broadcasted_iota(jnp.int32, (chips * own_cols, 2 * NZ * cols), 0)
    term = lax.broadcasted_iota(jnp.int32, (chips * own_cols, 2 * NZ * cols), 1) % (NZ * cols)
    place = (2 * (term // cols) + chip % 2) * own_cols + chip // 2 * cols + term % cols
    place = jnp.where(row == place, 1.0 / emb_scale, 0.0).astype(bf16).reshape(chips, own_cols, 2 * NZ * cols)
    hid_pair = jnp.concatenate([hid_own, hid_other, place], axis=2)

    up2, down2 = lax.ppermute(up1, "vocab", z_shift(1)), lax.ppermute(down1, "vocab", z_shift(-1))

    sums = segment_sum(after(packed, hid_own, scaled))
    sums = (sums * emb_scale).astype(f16).reshape(NZ, cols * vocab_rows // 128, 128)
    sums = lax.all_to_all(after(sums, up1, down1), "vocab", 0, 0, tiled=True).reshape(NZ * cols, vocab_rows)
    sums_high = sums.astype(bf16)
    sums_low = (sums.astype(f32) - sums_high.astype(f32)).astype(bf16)

    hid_sum = hid_terms(
        emb_cols, [z, z + 7, z + 1, z + 6, z + 2], [scaled, up1, down1, up2, down2]
    )
    up3 = lax.ppermute(up2, "vocab", z_shift(1))
    down3 = lax.ppermute(after(down2, hid_sum), "vocab", z_shift(-1))

    terms = jnp.concatenate([scaled, scaled_other, sums_high, sums_low])
    tied = jnp.einsum("kdt,tv->kdv", hid_pair, terms, preferred_element_type=f32)
    tied = after((tied * emb_scale).astype(f16), up2, down2)
    tied = lax.all_to_all(tied, "dp", 0, 0, axis_index_groups=same_core, tiled=True)

    half = tokens // 2
    up4, down4 = lax.ppermute(up3[:half], "vocab", z_shift(1)), lax.ppermute(down3[half:], "vocab", z_shift(-1))
    emb_last = [lax.dynamic_index_in_dim(emb_cols, (z + d) % NZ, 1) for d in (5, 3, 4)]
    hidden_grad = hid_terms(
        jnp.concatenate(emb_last, axis=1), [z * 0, z * 0 + 1, z * 0 + 2], [up3, down3, jnp.concatenate([up4, down4], axis=0)], hid_sum
    ).T

    embed_grad = (jnp.sum(after(tied, hidden_grad).astype(f32), axis=0) * (1.0 / emb_scale)).T
    return (token_loss, hidden_grad, embed_grad)


def solution(mesh):
    return jax.shard_map(
        per_device,
        mesh=mesh,
        in_specs=(P("vocab", None), P("dp", None), P("dp"), P("dp"), P("dp", "vocab")),
        out_specs=(P("dp"), P("dp", "vocab"), P("vocab", "dp")),
        check_vma=False,
    )
```

```python
import jax
import jax.numpy as jnp
from jax import lax
from jax.experimental import pallas as pl
from jax.experimental.pallas import tpu as pltpu
from jax.sharding import PartitionSpec as P

softcap = 30.0
bf16, f16, f32 = jnp.bfloat16, jnp.float16, jnp.float32
NZ, NX, NY = 8, 4, 4
DP = NX * NY * 2
emb_scale = 0.5


def z_shift(d):
    return [(i, (i + d) % NZ) for i in range(NZ)]


def z_xor(d):
    return [(i, i ^ d) for i in range(NZ)]


core_swap = [(i, i ^ 1) for i in range(DP)]


def segment_kernel(x_ref, o_ref):
    groups, rows, lanes = x_ref.shape
    cols = rows // 4 - 2
    r_iota = lax.broadcasted_iota(jnp.int32, (256, lanes), 0).astype(f32)
    q_iota = lax.broadcasted_iota(jnp.int32, (16, lanes), 0).astype(f32)

    def body(step, acc):
        left, right = [], []
        for n in range(4):
            x = x_ref[4 * step + n].astype(f32)
            for k in range(4):
                base = k * (cols + 2)
                hit = x[base + cols : base + cols + 1] == q_iota
                left.append(
                    jnp.concatenate(
                        [jnp.where(hit, x[base + c : base + c + 1], 0.0) for c in range(cols)], axis=0
                    ).astype(bf16)
                )
                right.append(jnp.where(x[base + cols + 1 : base + cols + 2] == r_iota, 1.0, 0.0).astype(bf16))
        left = jnp.concatenate(left, axis=1)
        right = jnp.concatenate(right, axis=1)
        return acc + lax.dot_general(left, right, (((1,), (1,)), ((), ())), preferred_element_type=f32)

    acc = lax.fori_loop(0, groups // 4, body, jnp.zeros((cols * 16, 256), f32))
    for c in range(cols):
        for q in range(16):
            o_ref[q // 2, c : c + 1, (q % 2) * 256 : (q % 2 + 1) * 256] = acc[c * 16 + q : c * 16 + q + 1]


def segment_sum(x):
    cols = x.shape[1] // 4 - 2
    return pl.pallas_call(
        segment_kernel,
        out_shape=jax.ShapeDtypeStruct((NZ, cols, 512), f32),
        in_specs=[pl.BlockSpec(memory_space=pltpu.VMEM)],
        out_specs=pl.BlockSpec(memory_space=pltpu.VMEM),
        compiler_params=pltpu.CompilerParams(vmem_limit_bytes=24 * 1024 * 1024),
        cost_estimate=pl.CostEstimate(flops=5_000_000_000, bytes_accessed=2_000_000, transcendentals=0),
    )(x)


same_core = [[2 * chip + c for chip in range(DP // 2)] for c in range(2)]
MB = 1024 * 1024


def after(x, *others):
    return lax.optimization_barrier((x,) + others)[0]


def hid_kernel(blocks, last, *refs):
    at_ref, emb_ref = refs[:2]
    block_refs = refs[2 : 2 + blocks]
    o_ref = refs[-1]
    rows = block_refs[0].shape[1]
    total = refs[2 + blocks][...] if last else None
    for i, block in enumerate(block_refs):
        term = jnp.dot(block[...], emb_ref[:, at_ref[i]].reshape(rows, -1), preferred_element_type=f32)
        total = term if total is None else total + term
    o_ref[...] = total.T if last else total


def hid_terms(emb_cols, shards, blocks, total=None):
    tokens, piece = blocks[0].shape[0], emb_cols.shape[-1]
    last = total is not None
    at = jnp.stack([s % NZ for s in shards])
    vmem = pl.BlockSpec(memory_space=pltpu.VMEM)
    args = [emb_cols, *blocks] + ([total] if last else [])
    return pl.pallas_call(
        lambda *refs: hid_kernel(len(blocks), last, *refs),
        out_shape=jax.ShapeDtypeStruct((piece, tokens) if last else (tokens, piece), f32),
        in_specs=[pl.BlockSpec(memory_space=pltpu.SMEM)] + [vmem] * len(args),
        out_specs=vmem,
        compiler_params=pltpu.CompilerParams(vmem_limit_bytes=28 * MB),
        cost_estimate=pl.CostEstimate(
            flops=2 * len(blocks) * tokens * tokens * piece, bytes_accessed=8 * MB, transcendentals=0
        ),
    )(at, *args)


def pack_kernel(grad_ref, ids_ref, o_ref):
    cols = o_ref.shape[1] // 4 - 2
    grad = grad_ref[...].astype(f32)
    ids = ids_ref[...]
    digits = [(ids // 256).astype(f32), (ids % 256).astype(f32)]
    for device in range(DP):
        b, a, c = device // 4, device // 2 % 2, device % 2
        base = ((a * 2 + c) * 8 + b) * cols
        rows = []
        for k in range(4):
            lanes = slice(k * 128, (k + 1) * 128)
            rows += [grad[base : base + cols, lanes]] + [d[:, lanes] for d in digits]
        o_ref[device] = jnp.concatenate(rows, axis=0).astype(bf16)


def pack_input(grad_t, ids):
    piece, tokens = grad_t.shape
    vmem = pl.BlockSpec(memory_space=pltpu.VMEM)
    return pl.pallas_call(
        pack_kernel,
        out_shape=jax.ShapeDtypeStruct((DP, 4 * (piece // DP + 2), tokens // 4), bf16),
        in_specs=[vmem, vmem],
        out_specs=vmem,
        compiler_params=pltpu.CompilerParams(vmem_limit_bytes=16 * MB),
        cost_estimate=pl.CostEstimate(flops=0, bytes_accessed=2 * MB, transcendentals=0),
    )(grad_t, ids.reshape(1, tokens))


def split_kernel(core_ref, x_ref, own_ref, other_ref):
    chips, own_cols, tokens = own_ref.shape
    x = x_ref[...].T.reshape(chips, 2, own_cols, tokens)
    first = core_ref[0] == 0
    own_ref[...] = jnp.where(first, x[:, 0], x[:, 1])
    other_ref[...] = jnp.where(first, x[:, 1], x[:, 0])


def split_hidden(hidden, core):
    tokens, width = hidden.shape
    own_cols = width // DP
    out = jax.ShapeDtypeStruct((DP // 2, own_cols, tokens), hidden.dtype)
    spec = pl.BlockSpec((4, own_cols, tokens), lambda i: (i, 0, 0))
    return pl.pallas_call(
        split_kernel,
        grid=(DP // 8,),
        out_shape=(out, out),
        in_specs=[pl.BlockSpec(memory_space=pltpu.SMEM), pl.BlockSpec((tokens, 8 * own_cols), lambda i: (0, i))],
        out_specs=(spec, spec),
        compiler_params=pltpu.CompilerParams(vmem_limit_bytes=24 * MB),
        cost_estimate=pl.CostEstimate(flops=0, bytes_accessed=9 * MB, transcendentals=0),
    )(core[None], hidden)


def per_device(embedding, hidden, targets, input_ids, input_grad):
    vocab_rows, width = embedding.shape
    tokens = hidden.shape[0]
    z = lax.axis_index("vocab")
    dp = lax.axis_index("dp")
    core, chip = dp % 2, dp // 2
    chips = DP // 2
    offset = z * vocab_rows
    piece = width // NZ
    own_cols = width // DP
    cols = piece // DP

    few = vocab_rows // DP
    emb_few = lax.dynamic_slice(embedding, (dp * few, 0), (few, width))
    emb_few = emb_few.reshape(few, NZ, piece).transpose(1, 0, 2)
    emb_few = lax.all_to_all(emb_few, "vocab", 0, 0, tiled=True)

    logits = jnp.einsum("td,vd->tv", hidden, embedding, preferred_element_type=f32)
    capped = softcap * jnp.tanh(logits / softcap)
    exponent = jnp.exp(capped)
    row_index = jnp.arange(vocab_rows, dtype=jnp.int32)
    target_hit = (row_index[None, :] == (targets - offset)[:, None]).astype(f32)
    stats = jnp.stack([jnp.sum(exponent, axis=1), jnp.sum(target_hit * capped, axis=1)])
    stats1 = stats + lax.ppermute(stats, "vocab", z_xor(1))
    emb_cols = lax.all_gather(after(emb_few, stats), "dp", axis=0, tiled=False)
    packed = pack_input(after(input_grad, stats).T, input_ids)
    stats1 = after(stats1, packed)
    stats2 = stats1 + lax.ppermute(stats1, "vocab", z_xor(2))
    packed = lax.all_to_all(packed, "dp", 0, 0, tiled=True)

    stats3 = stats2 + lax.ppermute(stats2, "vocab", z_xor(4))
    stats3 = after(stats3, packed)
    denominator, picked = stats3[0], stats3[1]
    token_loss = jnp.log(denominator) - picked
    scaled = (
        (exponent / denominator[:, None] - target_hit) * (1.0 - (capped / softcap) ** 2)
    ).astype(bf16)

    up1, down1 = lax.ppermute(scaled, "vocab", z_shift(1)), lax.ppermute(scaled, "vocab", z_shift(-1))
    scaled_other = lax.ppermute(scaled, "dp", core_swap)

    hid_own, hid_other = split_hidden(after(hidden, stats2), core)
    hid_other = lax.ppermute(hid_other, "dp", core_swap)
    row = lax.broadcasted_iota(jnp.int32, (chips * own_cols, 2 * NZ * cols), 0)
    term = lax.broadcasted_iota(jnp.int32, (chips * own_cols, 2 * NZ * cols), 1) % (NZ * cols)
    place = (2 * (term // cols) + chip % 2) * own_cols + chip // 2 * cols + term % cols
    place = jnp.where(row == place, 1.0 / emb_scale, 0.0).astype(bf16).reshape(chips, own_cols, 2 * NZ * cols)
    hid_pair = jnp.concatenate([hid_own, hid_other, place], axis=2)

    up2, down2 = lax.ppermute(up1, "vocab", z_shift(1)), lax.ppermute(down1, "vocab", z_shift(-1))

    sums = segment_sum(after(packed, hid_own, scaled))
    sums = (sums * emb_scale).astype(f16).reshape(NZ, cols * vocab_rows // 128, 128)
    sums = lax.all_to_all(after(sums, up1, down1), "vocab", 0, 0, tiled=True).reshape(NZ * cols, vocab_rows)
    sums_high = sums.astype(bf16)
    sums_low = (sums.astype(f32) - sums_high.astype(f32)).astype(bf16)

    hid_sum = hid_terms(
        emb_cols, [z, z + 7, z + 1, z + 6, z + 2], [scaled, up1, down1, up2, down2]
    )
    up3 = lax.ppermute(up2, "vocab", z_shift(1))
    down3 = lax.ppermute(after(down2, hid_sum), "vocab", z_shift(-1))

    terms = jnp.concatenate([scaled, scaled_other, sums_high, sums_low])
    tied = jnp.einsum("kdt,tv->kdv", hid_pair, terms, preferred_element_type=f32)
    tied = after((tied * emb_scale).astype(f16), up2, down2)
    tied = lax.all_to_all(tied, "dp", 0, 0, axis_index_groups=same_core, tiled=True)

    half = tokens // 2
    up4, down4 = lax.ppermute(up3[:half], "vocab", z_shift(1)), lax.ppermute(down3[half:], "vocab", z_shift(-1))
    emb_last = [lax.dynamic_index_in_dim(emb_cols, (z + d) % NZ, 1) for d in (5, 3, 4)]
    hidden_grad = hid_terms(
        jnp.concatenate(emb_last, axis=1), [z * 0, z * 0 + 1, z * 0 + 2], [up3, down3, jnp.concatenate([up4, down4], axis=0)], hid_sum
    ).T

    embed_grad = (jnp.sum(tied.astype(f32), axis=0) * (1.0 / emb_scale)).T
    return (token_loss, hidden_grad, embed_grad)


def solution(mesh):
    return jax.shard_map(
        per_device,
        mesh=mesh,
        in_specs=(P("vocab", None), P("dp", None), P("dp"), P("dp"), P("dp", "vocab")),
        out_specs=(P("dp"), P("dp", "vocab"), P("vocab", "dp")),
        check_vma=False,
    )
```
